32 devices in a mesh: grp: 4 (over y, x), row: 8 (over z, core).
Axes of the slice: x: 2, y: 2, z: 4, core: 2. Of those that a mesh axis runs over, the one named last changes fastest.
Arguments:
- field: float32 [4, 16, 512, 512], P(None, 'grp', None, 'row'), may hold values from -200 to 200
Outputs:
- factor: float32 [512, 512], replicated
- orthonormal: float32 [4, 16, 512, 512], P(None, 'grp', 'row')
The draws below stay inside these ranges and needn't reach their ends.
All inputs are finite; a program needn't handle non-finite values.
Results may differ from the reference program's by a relative error of at most 0.000073.
Values sent between devices are 32-bit elements; how exact they have to be, the bound alone decides.
A program may use at most 128 MiB of HBM per device.

```python
import math
import jax
import jax.numpy as jnp
from jax import lax

F = 4
N1 = 512
N2 = 512
N3 = 16


def draw_field(key, part):
    key_scale, key_core = jax.random.split(key, 2)
    ramp = 1.0 + 2.0 * jnp.arange(N3, dtype=jnp.float32) / max(N3 - 1, 1)
    scales = jnp.exp(jax.random.uniform(key_scale, (N1,), jnp.float32, 0.0, math.log(10.0)))
    core = jnp.clip(jax.random.normal(key_core, (F, N3, N2, N1), jnp.float32), -6.0, 6.0)
    return core * scales[None, None, None, :] * ramp[None, :, None, None]


def setup_inputs(seed: int = 0) -> dict:
    key_list = jax.random.split(jax.random.key(seed), 2)
    return {
        "field": draw_field(jax.random.fold_in(key_list[1], 71), 0),
    }


def reference(field):
    fcount, third, second, first = field.shape
    count = fcount * third * second

    def block_gram(block):
        mat = block.reshape(-1, first)
        return jnp.dot(mat.T.astype(jnp.float32), mat.astype(jnp.float32), precision=lax.Precision.HIGHEST, preferred_element_type=jnp.float32)
    gram = jnp.sum(lax.map(block_gram, field), axis=0) * (1.0 / count)
    factor = jnp.linalg.cholesky(gram)

    def block_solve(block):
        mat = block.reshape(-1, first)
        solved = lax.linalg.triangular_solve(factor, mat, left_side=False, lower=True, transpose_a=True)
        return solved.reshape(block.shape)
    orthonormal = lax.map(block_solve, field)
    return (factor, orthonormal)
```

```python
import functools

import jax
import jax.numpy as jnp
from jax import lax
from jax.experimental import pallas as pl
from jax.experimental.pallas import tpu as pltpu
from jax.sharding import PartitionSpec as P

MESH = pl.DeviceIdType.MESH
LANES = 128
HIGHEST = lax.Precision.HIGHEST
NT = (((1,), (1,)), ((), ()))


def offsets(order):
    blocks = order // LANES
    starts, at = [], 0
    for j in range(blocks):
        starts.append(at)
        at += order - j * LANES
    return starts, at


def share_kernel(
    n_row, n_grp, n_chunk, scale,
    field_ref, xt_ref, total_ref,
    send_ref, x_ref, gram_ref, pair_ref, half_ref, grp_ref, z_ref, sum_ref,
    a2a_send, a2a_recv, pair_sems, grp_send, grp_recv, z_send, z_recv, back_send, back_recv,
):
    row = lax.axis_index("row")
    grp = lax.axis_index("grp")
    core = lax.rem(row, 2)
    z = row // 2
    n_z = n_row // 2
    count, depth, width = field_ref.shape
    piece = width // n_row
    per_tile = LANES // piece
    order, columns = x_ref.shape
    chunk = columns // n_chunk
    tiles = chunk // LANES
    starts, used = offsets(order)

    barrier = pltpu.get_barrier_semaphore()
    for s in range(1, n_row):
        pl.semaphore_signal(
            barrier, inc=1, device_id={"row": lax.rem(row + s, n_row)}, device_id_type=MESH
        )
    for s in range(1, n_grp):
        pl.semaphore_signal(
            barrier, inc=1, device_id={"grp": lax.rem(grp + s, n_grp)}, device_id_type=MESH
        )

    lane = lax.broadcasted_iota(jnp.int32, (depth, LANES), 1)

    def pack(k):
        for d in range(n_row):
            source = d * piece // LANES * LANES
            shift = d * piece % LANES
            for t in range(k * tiles, (k + 1) * tiles):
                packed = None
                for j in range(per_tile):
                    value = field_ref[t * per_tile + j, :, source:source + LANES]
                    turn = (j * piece - shift) % LANES
                    if turn:
                        value = pltpu.roll(value, turn, 1)
                    packed = value if packed is None else jnp.where(lane >= j * piece, value, packed)
                send_ref[d, :, t * LANES:(t + 1) * LANES] = packed

    def a2a(k, s):
        to = lax.rem(row + s, n_row)
        return pltpu.make_async_remote_copy(
            src_ref=send_ref.at[to, :, pl.ds(k * chunk, chunk)],
            dst_ref=x_ref.at[pl.ds(pl.multiple_of(row * depth, depth), depth), pl.ds(k * chunk, chunk)],
            send_sem=a2a_send.at[k, s],
            recv_sem=a2a_recv.at[k, s],
            device_id={"row": to},
            device_id_type=MESH,
        )

    steps = list(range(1, n_row))
    for k in range(n_chunk):
        pack(k)
        if k == 0:
            pl.semaphore_wait(barrier, n_row + n_grp - 2)
        for s in steps:
            a2a(k, s).start()
    x_ref[pl.ds(pl.multiple_of(row * depth, depth), depth), :] = send_ref[row]

    for k in range(n_chunk):
        for s in steps:
            a2a(k, s).wait_recv()
        for j, start in enumerate(starts):
            rows = order - j * LANES
            product = lax.dot_general(
                x_ref[j * LANES:, k * chunk:(k + 1) * chunk],
                x_ref[j * LANES:(j + 1) * LANES, k * chunk:(k + 1) * chunk],
                NT, precision=HIGHEST, preferred_element_type=jnp.float32,
            )
            if k == 0:
                gram_ref[start:start + rows, :] = product
            else:
                gram_ref[start:start + rows, :] += product

    if used < gram_ref.shape[0]:
        gram_ref[used:, :] = jnp.zeros((gram_ref.shape[0] - used, LANES), jnp.float32)

    half = gram_ref.shape[0] // 2
    quarter = half // n_grp
    keep = pl.multiple_of(core * half, half)
    give = pl.multiple_of((1 - core) * half, half)
    sibling = z * 2 + 1 - core
    first = pltpu.make_async_remote_copy(
        src_ref=gram_ref.at[pl.ds(give, half)], dst_ref=pair_ref,
        send_sem=pair_sems.at[0], recv_sem=pair_sems.at[1],
        device_id={"row": sibling}, device_id_type=MESH,
    )
    first.start()
    for k in range(n_chunk):
        xt_ref[k * chunk:(k + 1) * chunk, :] = x_ref[:, k * chunk:(k + 1) * chunk].T
    first.wait_recv()
    half_ref[...] = gram_ref[pl.ds(keep, half), :] + pair_ref[...]

    second = []
    for s in range(1, n_grp):
        to = lax.rem(grp + s, n_grp)
        copy = pltpu.make_async_remote_copy(
            src_ref=half_ref.at[pl.ds(pl.multiple_of(to * quarter, quarter), quarter)],
            dst_ref=grp_ref.at[grp],
            send_sem=grp_send.at[s], recv_sem=grp_recv.at[s],
            device_id={"grp": to}, device_id_type=MESH,
        )
        copy.start()
        second.append(copy)
    grp_ref[grp] = half_ref[pl.ds(pl.multiple_of(grp * quarter, quarter), quarter), :]
    for copy in second:
        copy.wait_recv()
    z_ref[z] = functools.reduce(lambda a, b: a + b, [grp_ref[g] for g in range(n_grp)])

    third = []
    for s in range(1, n_z):
        to = lax.rem(z + s, n_z)
        copy = pltpu.make_async_remote_copy(
            src_ref=z_ref.at[z], dst_ref=z_ref.at[z],
            send_sem=z_send.at[s], recv_sem=z_recv.at[s],
            device_id={"row": to * 2 + core}, device_id_type=MESH,
        )
        copy.start()
        third.append(copy)
    for copy in third:
        copy.wait_recv()
    sum_ref[core, grp] = functools.reduce(lambda a, b: a + b, [z_ref[i] for i in range(n_z)]) * scale

    fourth = []
    for s in range(1, n_grp):
        to = lax.rem(grp + s, n_grp)
        copy = pltpu.make_async_remote_copy(
            src_ref=sum_ref.at[core, grp], dst_ref=sum_ref.at[core, grp],
            send_sem=back_send.at[s], recv_sem=back_recv.at[s],
            device_id={"grp": to}, device_id_type=MESH,
        )
        copy.start()
        fourth.append(copy)
    for copy in fourth:
        copy.wait_recv()
    last = pltpu.make_async_remote_copy(
        src_ref=sum_ref.at[core], dst_ref=sum_ref.at[core],
        send_sem=back_send.at[0], recv_sem=back_recv.at[0],
        device_id={"row": sibling}, device_id_type=MESH,
    )
    last.start()
    last.wait_recv()
    total_ref[...] = sum_ref[...]

    for k in range(n_chunk):
        for s in steps:
            a2a(k, s).wait_send()
    for copy in [first, *second, *third, *fourth, last]:
        copy.wait_send()


def share(pieces, scale):
    n_row, n_grp = lax.axis_size("row"), lax.axis_size("grp")
    count, depth, width = pieces.shape
    order = depth * n_row
    columns = count * (width // n_row)
    n_chunk = min(4, columns // LANES)
    _, rows = offsets(order)
    quantum = 2 * n_grp * 8
    rows = -(-rows // quantum) * quantum
    quarter = rows // (2 * n_grp)
    n_z = n_row // 2
    f32 = jnp.float32
    dma = pltpu.SemaphoreType.DMA
    vmem = pl.BlockSpec(memory_space=pltpu.VMEM)
    xt, total = pl.pallas_call(
        functools.partial(share_kernel, n_row, n_grp, n_chunk, scale),
        out_shape=[
            jax.ShapeDtypeStruct((columns, order), f32),
            jax.ShapeDtypeStruct((2, n_grp, quarter, LANES), f32),
        ],
        in_specs=[vmem],
        out_specs=[vmem, vmem],
        scratch_shapes=[
            pltpu.VMEM((n_row, depth, columns), f32),
            pltpu.VMEM((order, columns), f32),
            pltpu.VMEM((rows, LANES), f32),
            pltpu.VMEM((rows // 2, LANES), f32),
            pltpu.VMEM((rows // 2, LANES), f32),
            pltpu.VMEM((n_grp, quarter, LANES), f32),
            pltpu.VMEM((n_z, quarter, LANES), f32),
            pltpu.VMEM((2, n_grp, quarter, LANES), f32),
            dma((n_chunk, n_row)), dma((n_chunk, n_row)),
            dma((2,)),
            dma((n_grp,)), dma((n_grp,)),
            dma((n_z,)), dma((n_z,)),
            dma((n_grp,)), dma((n_grp,)),
        ],
        compiler_params=pltpu.CompilerParams(
            collective_id=0, has_side_effects=True, vmem_limit_bytes=48 * 2**20
        ),
    )(pieces)
    return xt, total.reshape(rows, LANES)


def per_device(field):
    fields, third, second, first = field.shape
    count = fields * third * lax.axis_size("grp") * second
    order = first * lax.axis_size("row")
    pieces = jnp.swapaxes(field, 2, 3).reshape(fields * third, first, second)
    xt, packed = share(pieces, 1.0 / count)
    starts, _ = offsets(order)
    blocks = [
        jnp.pad(packed[start:start + order - j * LANES], ((j * LANES, 0), (0, 0)))
        for j, start in enumerate(starts)
    ]
    factor = jnp.linalg.cholesky(jnp.concatenate(blocks, axis=1), symmetrize_input=False)
    solved = lax.linalg.triangular_solve(factor, xt, left_side=False, lower=True, transpose_a=True)
    return (factor, solved.reshape(fields, third, second // lax.axis_size("row"), order))


def solution(mesh):
    return jax.shard_map(
        per_device,
        mesh=mesh,
        in_specs=(P(None, "grp", None, "row"),),
        out_specs=(P(), P(None, "grp", "row", None)),
        check_vma=False,
    )
```

```python
import functools

import jax
import jax.numpy as jnp
from jax import lax
from jax.experimental import pallas as pl
from jax.experimental.pallas import tpu as pltpu
from jax.sharding import PartitionSpec as P

MESH = pl.DeviceIdType.MESH
LANES = 128
HIGHEST = lax.Precision.HIGHEST
NT = (((1,), (1,)), ((), ()))


def offsets(order):
    blocks = order // LANES
    starts, at = [], 0
    for j in range(blocks):
        starts.append(at)
        at += order - j * LANES
    return starts, at


def share_kernel(
    n_row, n_grp, n_chunk, scale,
    field_ref, xt_ref, total_ref,
    send_ref, x_ref, gram_ref, pair_ref, half_ref, grp_ref, z_ref, sum_ref,
    a2a_send, a2a_recv, pair_sems, grp_send, grp_recv, z_send, z_recv, back_send, back_recv,
):
    row = lax.axis_index("row")
    grp = lax.axis_index("grp")
    core = lax.rem(row, 2)
    z = row // 2
    n_z = n_row // 2
    count, depth, width = field_ref.shape
    piece = width // n_row
    per_tile = LANES // piece
    order, columns = x_ref.shape
    chunk = columns // n_chunk
    tiles = chunk // LANES
    starts, used = offsets(order)

    barrier = pltpu.get_barrier_semaphore()
    for s in range(1, n_row):
        pl.semaphore_signal(
            barrier, inc=1, device_id={"row": lax.rem(row + s, n_row)}, device_id_type=MESH
        )
    for s in range(1, n_grp):
        pl.semaphore_signal(
            barrier, inc=1, device_id={"grp": lax.rem(grp + s, n_grp)}, device_id_type=MESH
        )

    lane = lax.broadcasted_iota(jnp.int32, (depth, LANES), 1)

    def pack(k):
        for d in range(n_row):
            source = d * piece // LANES * LANES
            shift = d * piece % LANES
            for t in range(k * tiles, (k + 1) * tiles):
                packed = None
                for j in range(per_tile):
                    value = field_ref[t * per_tile + j, :, source:source + LANES]
                    turn = (j * piece - shift) % LANES
                    if turn:
                        value = pltpu.roll(value, turn, 1)
                    packed = value if packed is None else jnp.where(lane >= j * piece, value, packed)
                send_ref[d, :, t * LANES:(t + 1) * LANES] = packed

    def a2a(k, s):
        to = lax.rem(row + s, n_row)
        return pltpu.make_async_remote_copy(
            src_ref=send_ref.at[to, :, pl.ds(k * chunk, chunk)],
            dst_ref=x_ref.at[pl.ds(pl.multiple_of(row * depth, depth), depth), pl.ds(k * chunk, chunk)],
            send_sem=a2a_send.at[k, s],
            recv_sem=a2a_recv.at[k, s],
            device_id={"row": to},
            device_id_type=MESH,
        )

    steps = list(range(1, n_row))
    for k in range(n_chunk):
        pack(k)
        if k == 0:
            pl.semaphore_wait(barrier, n_row + n_grp - 2)
        for s in steps:
            a2a(k, s).start()
    x_ref[pl.ds(pl.multiple_of(row * depth, depth), depth), :] = send_ref[row]

    for k in range(n_chunk):
        for s in steps:
            a2a(k, s).wait_recv()
        for j, start in enumerate(starts):
            rows = order - j * LANES
            product = lax.dot_general(
                x_ref[j * LANES:, k * chunk:(k + 1) * chunk],
                x_ref[j * LANES:(j + 1) * LANES, k * chunk:(k + 1) * chunk],
                NT, precision=HIGHEST, preferred_element_type=jnp.float32,
            )
            if k == 0:
                gram_ref[start:start + rows, :] = product
            else:
                gram_ref[start:start + rows, :] += product

    if used < gram_ref.shape[0]:
        gram_ref[used:, :] = jnp.zeros((gram_ref.shape[0] - used, LANES), jnp.float32)

    half = gram_ref.shape[0] // 2
    quarter = half // n_grp
    keep = pl.multiple_of(core * half, half)
    give = pl.multiple_of((1 - core) * half, half)
    sibling = z * 2 + 1 - core
    first = pltpu.make_async_remote_copy(
        src_ref=gram_ref.at[pl.ds(give, half)], dst_ref=pair_ref,
        send_sem=pair_sems.at[0], recv_sem=pair_sems.at[1],
        device_id={"row": sibling}, device_id_type=MESH,
    )
    first.start()
    for k in range(n_chunk):
        xt_ref[k * chunk:(k + 1) * chunk, :] = x_ref[:, k * chunk:(k + 1) * chunk].T
    first.wait_recv()
    half_ref[...] = gram_ref[pl.ds(keep, half), :] + pair_ref[...]

    second = []
    for s in range(1, n_grp):
        to = lax.rem(grp + s, n_grp)
        copy = pltpu.make_async_remote_copy(
            src_ref=half_ref.at[pl.ds(pl.multiple_of(to * quarter, quarter), quarter)],
            dst_ref=grp_ref.at[grp],
            send_sem=grp_send.at[s], recv_sem=grp_recv.at[s],
            device_id={"grp": to}, device_id_type=MESH,
        )
        copy.start()
        second.append(copy)
    grp_ref[grp] = half_ref[pl.ds(pl.multiple_of(grp * quarter, quarter), quarter), :]
    for copy in second:
        copy.wait_recv()
    z_ref[z] = functools.reduce(lambda a, b: a + b, [grp_ref[g] for g in range(n_grp)])

    third = []
    for s in range(1, n_z):
        to = lax.rem(z + s, n_z)
        copy = pltpu.make_async_remote_copy(
            src_ref=z_ref.at[z], dst_ref=z_ref.at[z],
            send_sem=z_send.at[s], recv_sem=z_recv.at[s],
            device_id={"row": to * 2 + core}, device_id_type=MESH,
        )
        copy.start()
        third.append(copy)
    for copy in third:
        copy.wait_recv()
    sum_ref[core, grp] = functools.reduce(lambda a, b: a + b, [z_ref[i] for i in range(n_z)]) * scale

    fourth = []
    for s in range(1, n_grp):
        to = lax.rem(grp + s, n_grp)
        copy = pltpu.make_async_remote_copy(
            src_ref=sum_ref.at[core, grp], dst_ref=sum_ref.at[core, grp],
            send_sem=back_send.at[s], recv_sem=back_recv.at[s],
            device_id={"grp": to}, device_id_type=MESH,
        )
        copy.start()
        fourth.append(copy)
    for copy in fourth:
        copy.wait_recv()
    last = pltpu.make_async_remote_copy(
        src_ref=sum_ref.at[core], dst_ref=sum_ref.at[core],
        send_sem=back_send.at[0], recv_sem=back_recv.at[0],
        device_id={"row": sibling}, device_id_type=MESH,
    )
    last.start()
    last.wait_recv()
    total_ref[...] = sum_ref[...]

    for k in range(n_chunk):
        for s in steps:
            a2a(k, s).wait_send()
    for copy in [first, *second, *third, *fourth, last]:
        copy.wait_send()


def share(pieces, scale):
    n_row, n_grp = lax.axis_size("row"), lax.axis_size("grp")
    count, depth, width = pieces.shape
    order = depth * n_row
    columns = count * (width // n_row)
    n_chunk = min(4, columns // LANES)
    _, rows = offsets(order)
    quantum = 2 * n_grp * 8
    rows = -(-rows // quantum) * quantum
    quarter = rows // (2 * n_grp)
    n_z = n_row // 2
    f32 = jnp.float32
    dma = pltpu.SemaphoreType.DMA
    vmem = pl.BlockSpec(memory_space=pltpu.VMEM)
    xt, total = pl.pallas_call(
        functools.partial(share_kernel, n_row, n_grp, n_chunk, scale),
        out_shape=[
            jax.ShapeDtypeStruct((columns, order), f32),
            jax.ShapeDtypeStruct((2, n_grp, quarter, LANES), f32),
        ],
        in_specs=[vmem],
        out_specs=[vmem, vmem],
        scratch_shapes=[
            pltpu.VMEM((n_row, depth, columns), f32),
            pltpu.VMEM((order, columns), f32),
            pltpu.VMEM((rows, LANES), f32),
            pltpu.VMEM((rows // 2, LANES), f32),
            pltpu.VMEM((rows // 2, LANES), f32),
            pltpu.VMEM((n_grp, quarter, LANES), f32),
            pltpu.VMEM((n_z, quarter, LANES), f32),
            pltpu.VMEM((2, n_grp, quarter, LANES), f32),
            dma((n_chunk, n_row)), dma((n_chunk, n_row)),
            dma((2,)),
            dma((n_grp,)), dma((n_grp,)),
            dma((n_z,)), dma((n_z,)),
            dma((n_grp,)), dma((n_grp,)),
        ],
        compiler_params=pltpu.CompilerParams(
            collective_id=0, has_side_effects=True, vmem_limit_bytes=48 * 2**20
        ),
    )(pieces)
    return xt, total.reshape(rows, LANES)


def eliminate(work_ref, upper_ref, inverse_ref):
    sub = lax.broadcasted_iota(jnp.int32, (8, LANES), 0)
    full = (8, LANES)

    def splat_rows(value):
        return [jnp.broadcast_to(value[i:i + 1, :], full) for i in range(8)]

    def gather_rows(rows):
        out = rows[0]
        for i in range(1, 8):
            out = jnp.where(sub == i, rows[i], out)
        return out

    for j in range(LANES // 8):
        at = 8 * j
        left = work_ref[at:at + 8, :LANES]
        right = work_ref[at:at + 8, LANES:]
        d = [[None] * 8 for _ in range(8)]
        for m in range(8):
            spread = jnp.broadcast_to(left[:, at + m:at + m + 1], full)
            for i in range(m, 8):
                d[i][m] = jnp.broadcast_to(spread[i:i + 1, :], full)
        a = splat_rows(left)
        e = splat_rows(right)
        inv = [None] * 8
        for k in range(8):
            inv[k] = lax.rsqrt(d[k][k])
            for i in range(k + 1, 8):
                d[i][k] = d[i][k] * inv[k]
            for m in range(k + 1, 8):
                for i in range(m, 8):
                    d[i][m] = d[i][m] - d[i][k] * d[m][k]
            a[k] = a[k] * inv[k]
            e[k] = e[k] * inv[k]
            for i in range(k + 1, 8):
                a[i] = a[i] - d[i][k] * a[k]
                e[i] = e[i] - d[i][k] * e[k]
        upper_ref[at:at + 8, :] = gather_rows(a)
        inverse_ref[at:at + 8, :] = gather_rows(e)
        for k in reversed(range(8)):
            a[k] = a[k] * inv[k]
            e[k] = e[k] * inv[k]
            for i in range(k):
                a[i] = a[i] - d[k][i] * a[k]
                e[i] = e[i] - d[k][i] * e[k]
        for g in range(j + 1, LANES // 8):
            left = work_ref[8 * g:8 * g + 8, :LANES]
            right = work_ref[8 * g:8 * g + 8, LANES:]
            spreads = [jnp.broadcast_to(left[:, at + k:at + k + 1], full) for k in range(8)]
            for k in range(8):
                left = left - spreads[k] * a[k]
                right = right - spreads[k] * e[k]
            work_ref[8 * g:8 * g + 8, :LANES] = left
            work_ref[8 * g:8 * g + 8, LANES:] = right


def solve_kernel(total_ref, xt_ref, factor_ref, out_ref, gram_ref, work_ref, upper_ref, inverse_ref):
    order = factor_ref.shape[0]
    starts, used = offsets(order)
    dot = functools.partial(
        lax.dot_general, dimension_numbers=NT, precision=HIGHEST, preferred_element_type=jnp.float32
    )
    r = lax.broadcasted_iota(jnp.int32, (LANES, LANES), 0)
    c = lax.broadcasted_iota(jnp.int32, (LANES, LANES), 1)
    blocks = order // LANES
    gram_ref[...] = total_ref[:used, :]
    for b in range(blocks):
        lo, hi = b * LANES, (b + 1) * LANES
        start = starts[b]
        work_ref[b, :, :LANES] = gram_ref[start:start + LANES, :]
        work_ref[b, :, LANES:] = jnp.where(r == c, 1.0, 0.0)
        eliminate(work_ref.at[b], upper_ref.at[b], inverse_ref.at[b])
        inverse = inverse_ref[b]
        if hi < order:
            below = dot(gram_ref[start + LANES:start + order - lo, :], inverse)
            factor_ref[hi:, lo:hi] = below
            for j in range(b + 1, blocks):
                skip = (j - b - 1) * LANES
                here = slice(starts[j], starts[j] + order - j * LANES)
                gram_ref[here, :] -= dot(below[skip:, :], below[skip:skip + LANES, :])
        factor_ref[lo:hi, lo:hi] = jnp.where(r >= c, upper_ref[b].T, 0.0)
        if b:
            factor_ref[:lo, lo:hi] = jnp.zeros((lo, LANES), jnp.float32)
        source = xt_ref if b == 0 else out_ref
        solved = dot(source[:, lo:hi], inverse)
        out_ref[:, lo:hi] = solved
        if hi < order:
            out_ref[:, hi:] = source[:, hi:] - dot(solved, below)


def factor_and_solve(packed, xt):
    columns, order = xt.shape
    _, used = offsets(order)
    f32 = jnp.float32
    blocks = order // LANES
    vmem = pl.BlockSpec(memory_space=pltpu.VMEM)
    return pl.pallas_call(
        solve_kernel,
        out_shape=[
            jax.ShapeDtypeStruct((order, order), f32),
            jax.ShapeDtypeStruct((columns, order), f32),
        ],
        in_specs=[vmem, vmem],
        out_specs=[vmem, vmem],
        scratch_shapes=[
            pltpu.VMEM((used, LANES), f32),
            pltpu.VMEM((blocks, LANES, 2 * LANES), f32),
            pltpu.VMEM((blocks, LANES, LANES), f32),
            pltpu.VMEM((blocks, LANES, LANES), f32),
        ],
        compiler_params=pltpu.CompilerParams(vmem_limit_bytes=48 * 2**20),
    )(packed, xt)


def per_device(field):
    fields, third, second, first = field.shape
    count = fields * third * lax.axis_size("grp") * second
    order = first * lax.axis_size("row")
    pieces = jnp.swapaxes(field, 2, 3).reshape(fields * third, first, second)
    xt, packed = share(pieces, 1.0 / count)
    factor, solved = factor_and_solve(packed, xt)
    return (factor, solved.reshape(fields, third, second // lax.axis_size("row"), order))


def solution(mesh):
    return jax.shard_map(
        per_device,
        mesh=mesh,
        in_specs=(P(None, "grp", None, "row"),),
        out_specs=(P(), P(None, "grp", "row", None)),
        check_vma=False,
    )
```

```python
import functools

import jax
import jax.numpy as jnp
from jax import lax
from jax.experimental import pallas as pl
from jax.experimental.pallas import tpu as pltpu
from jax.sharding import PartitionSpec as P

MESH = pl.DeviceIdType.MESH
LANES = 128
HIGHEST = lax.Precision.HIGHEST
NT = (((1,), (1,)), ((), ()))


def offsets(order):
    blocks = order // LANES
    starts, at = [], 0
    for j in range(blocks):
        starts.append(at)
        at += order - j * LANES
    return starts, at


def share_kernel(
    n_row, n_grp, n_chunk, scale,
    field_ref, xt_ref, total_ref,
    send_ref, x_ref, gram_ref, pair_ref, half_ref, grp_ref, z_ref, sum_ref,
    a2a_send, a2a_recv, pair_sems, grp_send, grp_recv, z_send, z_recv, back_send, back_recv,
):
    row = lax.axis_index("row")
    grp = lax.axis_index("grp")
    core = lax.rem(row, 2)
    z = row // 2
    n_z = n_row // 2
    count, depth, width = field_ref.shape
    piece = width // n_row
    per_tile = LANES // piece
    order, columns = x_ref.shape
    chunk = columns // n_chunk
    tiles = chunk // LANES
    starts, used = offsets(order)

    barrier = pltpu.get_barrier_semaphore()
    for s in range(1, n_row):
        pl.semaphore_signal(
            barrier, inc=1, device_id={"row": lax.rem(row + s, n_row)}, device_id_type=MESH
        )
    for s in range(1, n_grp):
        pl.semaphore_signal(
            barrier, inc=1, device_id={"grp": lax.rem(grp + s, n_grp)}, device_id_type=MESH
        )

    lane = lax.broadcasted_iota(jnp.int32, (depth, LANES), 1)

    def pack(k):
        for d in range(n_row):
            source = d * piece // LANES * LANES
            shift = d * piece % LANES
            for t in range(k * tiles, (k + 1) * tiles):
                packed = None
                for j in range(per_tile):
                    value = field_ref[t * per_tile + j, :, source:source + LANES]
                    turn = (j * piece - shift) % LANES
                    if turn:
                        value = pltpu.roll(value, turn, 1)
                    packed = value if packed is None else jnp.where(lane >= j * piece, value, packed)
                send_ref[d, :, t * LANES:(t + 1) * LANES] = packed

    def a2a(k, s):
        to = lax.rem(row + s, n_row)
        return pltpu.make_async_remote_copy(
            src_ref=send_ref.at[to, :, pl.ds(k * chunk, chunk)],
            dst_ref=x_ref.at[pl.ds(pl.multiple_of(row * depth, depth), depth), pl.ds(k * chunk, chunk)],
            send_sem=a2a_send.at[k, s],
            recv_sem=a2a_recv.at[k, s],
            device_id={"row": to},
            device_id_type=MESH,
        )

    steps = list(range(1, n_row))
    for k in range(n_chunk):
        pack(k)
        if k == 0:
            pl.semaphore_wait(barrier, n_row + n_grp - 2)
        for s in steps:
            a2a(k, s).start()
    x_ref[pl.ds(pl.multiple_of(row * depth, depth), depth), :] = send_ref[row]

    for k in range(n_chunk):
        for s in steps:
            a2a(k, s).wait_recv()
        for j, start in enumerate(starts):
            rows = order - j * LANES
            product = lax.dot_general(
                x_ref[j * LANES:, k * chunk:(k + 1) * chunk],
                x_ref[j * LANES:(j + 1) * LANES, k * chunk:(k + 1) * chunk],
                NT, precision=HIGHEST, preferred_element_type=jnp.float32,
            )
            if k == 0:
                gram_ref[start:start + rows, :] = product
            else:
                gram_ref[start:start + rows, :] += product

    if used < gram_ref.shape[0]:
        gram_ref[used:, :] = jnp.zeros((gram_ref.shape[0] - used, LANES), jnp.float32)

    half = gram_ref.shape[0] // 2
    quarter = half // n_grp
    keep = pl.multiple_of(core * half, half)
    give = pl.multiple_of((1 - core) * half, half)
    sibling = z * 2 + 1 - core
    first = pltpu.make_async_remote_copy(
        src_ref=gram_ref.at[pl.ds(give, half)], dst_ref=pair_ref,
        send_sem=pair_sems.at[0], recv_sem=pair_sems.at[1],
        device_id={"row": sibling}, device_id_type=MESH,
    )
    first.start()
    for k in range(n_chunk):
        xt_ref[k * chunk:(k + 1) * chunk, :] = x_ref[:, k * chunk:(k + 1) * chunk].T
    first.wait_recv()
    half_ref[...] = gram_ref[pl.ds(keep, half), :] + pair_ref[...]

    second = []
    for s in range(1, n_grp):
        to = lax.rem(grp + s, n_grp)
        copy = pltpu.make_async_remote_copy(
            src_ref=half_ref.at[pl.ds(pl.multiple_of(to * quarter, quarter), quarter)],
            dst_ref=grp_ref.at[grp],
            send_sem=grp_send.at[s], recv_sem=grp_recv.at[s],
            device_id={"grp": to}, device_id_type=MESH,
        )
        copy.start()
        second.append(copy)
    grp_ref[grp] = half_ref[pl.ds(pl.multiple_of(grp * quarter, quarter), quarter), :]
    for copy in second:
        copy.wait_recv()
    z_ref[z] = functools.reduce(lambda a, b: a + b, [grp_ref[g] for g in range(n_grp)])

    third = []
    for s in range(1, n_z):
        to = lax.rem(z + s, n_z)
        copy = pltpu.make_async_remote_copy(
            src_ref=z_ref.at[z], dst_ref=z_ref.at[z],
            send_sem=z_send.at[s], recv_sem=z_recv.at[s],
            device_id={"row": to * 2 + core}, device_id_type=MESH,
        )
        copy.start()
        third.append(copy)
    for copy in third:
        copy.wait_recv()
    sum_ref[core, grp] = functools.reduce(lambda a, b: a + b, [z_ref[i] for i in range(n_z)]) * scale

    fourth = []
    for s in range(1, n_grp):
        to = lax.rem(grp + s, n_grp)
        copy = pltpu.make_async_remote_copy(
            src_ref=sum_ref.at[core, grp], dst_ref=sum_ref.at[core, grp],
            send_sem=back_send.at[s], recv_sem=back_recv.at[s],
            device_id={"grp": to}, device_id_type=MESH,
        )
        copy.start()
        fourth.append(copy)
    for copy in fourth:
        copy.wait_recv()
    last = pltpu.make_async_remote_copy(
        src_ref=sum_ref.at[core], dst_ref=sum_ref.at[core],
        send_sem=back_send.at[0], recv_sem=back_recv.at[0],
        device_id={"row": sibling}, device_id_type=MESH,
    )
    last.start()
    last.wait_recv()
    total_ref[...] = sum_ref[...]

    for k in range(n_chunk):
        for s in steps:
            a2a(k, s).wait_send()
    for copy in [first, *second, *third, *fourth, last]:
        copy.wait_send()


def share(pieces, scale):
    n_row, n_grp = lax.axis_size("row"), lax.axis_size("grp")
    count, depth, width = pieces.shape
    order = depth * n_row
    columns = count * (width // n_row)
    n_chunk = min(4, columns // LANES)
    _, rows = offsets(order)
    quantum = 2 * n_grp * 8
    rows = -(-rows // quantum) * quantum
    quarter = rows // (2 * n_grp)
    n_z = n_row // 2
    f32 = jnp.float32
    dma = pltpu.SemaphoreType.DMA
    vmem = pl.BlockSpec(memory_space=pltpu.VMEM)
    xt, total = pl.pallas_call(
        functools.partial(share_kernel, n_row, n_grp, n_chunk, scale),
        out_shape=[
            jax.ShapeDtypeStruct((columns, order), f32),
            jax.ShapeDtypeStruct((2, n_grp, quarter, LANES), f32),
        ],
        in_specs=[vmem],
        out_specs=[vmem, vmem],
        scratch_shapes=[
            pltpu.VMEM((n_row, depth, columns), f32),
            pltpu.VMEM((order, columns), f32),
            pltpu.VMEM((rows, LANES), f32),
            pltpu.VMEM((rows // 2, LANES), f32),
            pltpu.VMEM((rows // 2, LANES), f32),
            pltpu.VMEM((n_grp, quarter, LANES), f32),
            pltpu.VMEM((n_z, quarter, LANES), f32),
            pltpu.VMEM((2, n_grp, quarter, LANES), f32),
            dma((n_chunk, n_row)), dma((n_chunk, n_row)),
            dma((2,)),
            dma((n_grp,)), dma((n_grp,)),
            dma((n_z,)), dma((n_z,)),
            dma((n_grp,)), dma((n_grp,)),
        ],
        compiler_params=pltpu.CompilerParams(
            collective_id=0, has_side_effects=True, vmem_limit_bytes=48 * 2**20
        ),
    )(pieces)
    return xt, total.reshape(rows, LANES)


def eliminate(work_ref, upper_ref, inverse_ref, spread_ref):
    sub = lax.broadcasted_iota(jnp.int32, (8, LANES), 0)
    full = (8, LANES)

    def gather_rows(rows):
        out = rows[0]
        for i in range(1, 8):
            out = jnp.where(sub == i, rows[i], out)
        return out

    def update(g, at, a, e):
        left = work_ref[8 * g:8 * g + 8, :LANES]
        right = work_ref[8 * g:8 * g + 8, LANES:]
        spreads = [jnp.broadcast_to(left[:, at + k:at + k + 1], full) for k in range(8)]
        for k in range(8):
            left = left - spreads[k] * a[k]
            right = right - spreads[k] * e[k]
        work_ref[8 * g:8 * g + 8, :LANES] = left
        work_ref[8 * g:8 * g + 8, LANES:] = right

    pending = []
    groups = LANES // 8
    for j in range(groups):
        at = 8 * j
        left = work_ref[at:at + 8, :LANES]
        d = [[None] * 8 for _ in range(8)]
        for m in range(8):
            spread = jnp.broadcast_to(left[:, at + m:at + m + 1], full)
            spread_ref[j % 2, 8 * m:8 * m + 8, :] = spread
            for i in range(m, 8):
                d[i][m] = jnp.broadcast_to(spread_ref[j % 2, 8 * m + i:8 * m + i + 1, :], full)
        a = [jnp.broadcast_to(work_ref[at + i:at + i + 1, :LANES], full) for i in range(8)]
        e = [jnp.broadcast_to(work_ref[at + i:at + i + 1, LANES:], full) for i in range(8)]
        inv = [None] * 8
        share_of = -(-len(pending) // 8)
        for k in range(8):
            inv[k] = lax.rsqrt(d[k][k])
            for i in range(k + 1, 8):
                d[i][k] = d[i][k] * inv[k]
            for m in range(k + 1, 8):
                for i in range(m, 8):
                    d[i][m] = d[i][m] - d[i][k] * d[m][k]
            a[k] = a[k] * inv[k]
            e[k] = e[k] * inv[k]
            for i in range(k + 1, 8):
                a[i] = a[i] - d[i][k] * a[k]
                e[i] = e[i] - d[i][k] * e[k]
            for step in pending[k * share_of:(k + 1) * share_of]:
                update(*step)
        upper_ref[at:at + 8, :] = gather_rows(a)
        inverse_ref[at:at + 8, :] = gather_rows(e)
        for k in reversed(range(8)):
            a[k] = a[k] * inv[k]
            e[k] = e[k] * inv[k]
            for i in range(k):
                a[i] = a[i] - d[k][i] * a[k]
                e[i] = e[i] - d[k][i] * e[k]
        end = groups // 2 if j < groups // 2 else groups
        if j + 1 < end:
            update(j + 1, at, a, e)
        pending = [(g, at, tuple(a), tuple(e)) for g in range(j + 2, end)]
        if j + 1 == groups // 2:
            cut = LANES // 2
            turned = upper_ref[:cut, :].T[cut:, :]
            work_ref[cut:, :LANES] -= jnp.dot(
                turned, upper_ref[:cut, :], precision=HIGHEST, preferred_element_type=jnp.float32
            )
            work_ref[cut:, LANES:] -= jnp.dot(
                turned, inverse_ref[:cut, :], precision=HIGHEST, preferred_element_type=jnp.float32
            )


def solve_kernel(total_ref, xt_ref, factor_ref, out_ref, gram_ref, work_ref, upper_ref, inverse_ref, spread_ref):
    order = factor_ref.shape[0]
    starts, used = offsets(order)
    dot = functools.partial(
        lax.dot_general, dimension_numbers=NT, precision=HIGHEST, preferred_element_type=jnp.float32
    )
    r = lax.broadcasted_iota(jnp.int32, (LANES, LANES), 0)
    c = lax.broadcasted_iota(jnp.int32, (LANES, LANES), 1)
    blocks = order // LANES
    gram_ref[...] = total_ref[:used, :]
    for b in range(blocks):
        lo, hi = b * LANES, (b + 1) * LANES
        start = starts[b]
        work_ref[b, :, :LANES] = gram_ref[start:start + LANES, :]
        work_ref[b, :, LANES:] = jnp.where(r == c, 1.0, 0.0)
        eliminate(work_ref.at[b], upper_ref.at[b], inverse_ref.at[b], spread_ref)
        inverse = inverse_ref[b]
        if hi < order:
            below = []
            for i in range(b + 1, blocks):
                here = start + (i - b) * LANES
                part = dot(gram_ref[here:here + LANES, :], inverse)
                factor_ref[i * LANES:(i + 1) * LANES, lo:hi] = part
                below.append(part)
                for j in range(b + 1, i + 1):
                    here = starts[j] + (i - j) * LANES
                    gram_ref[here:here + LANES, :] -= dot(part, below[j - b - 1])
        factor_ref[lo:hi, lo:hi] = jnp.where(r >= c, upper_ref[b].T, 0.0)
        if b:
            factor_ref[:lo, lo:hi] = jnp.zeros((lo, LANES), jnp.float32)
        source = xt_ref if b == 0 else out_ref
        solved = dot(source[:, lo:hi], inverse)
        out_ref[:, lo:hi] = solved
        if hi < order:
            for j in range(b + 1, blocks):
                there = slice(j * LANES, (j + 1) * LANES)
                out_ref[:, there] = source[:, there] - dot(solved, below[j - b - 1])


def factor_and_solve(packed, xt):
    columns, order = xt.shape
    _, used = offsets(order)
    f32 = jnp.float32
    blocks = order // LANES
    vmem = pl.BlockSpec(memory_space=pltpu.VMEM)
    return pl.pallas_call(
        solve_kernel,
        out_shape=[
            jax.ShapeDtypeStruct((order, order), f32),
            jax.ShapeDtypeStruct((columns, order), f32),
        ],
        in_specs=[vmem, vmem],
        out_specs=[vmem, vmem],
        scratch_shapes=[
            pltpu.VMEM((used, LANES), f32),
            pltpu.VMEM((blocks, LANES, 2 * LANES), f32),
            pltpu.VMEM((blocks, LANES, LANES), f32),
            pltpu.VMEM((blocks, LANES, LANES), f32),
            pltpu.VMEM((2, 64, LANES), f32),
        ],
        compiler_params=pltpu.CompilerParams(vmem_limit_bytes=48 * 2**20),
    )(packed, xt)


def per_device(field):
    fields, third, second, first = field.shape
    count = fields * third * lax.axis_size("grp") * second
    order = first * lax.axis_size("row")
    pieces = jnp.swapaxes(field, 2, 3).reshape(fields * third, first, second)
    xt, packed = share(pieces, 1.0 / count)
    factor, solved = factor_and_solve(packed, xt)
    return (factor, solved.reshape(fields, third, second // lax.axis_size("row"), order))


def solution(mesh):
    return jax.shard_map(
        per_device,
        mesh=mesh,
        in_specs=(P(None, "grp", None, "row"),),
        out_specs=(P(), P(None, "grp", "row", None)),
        check_vma=False,
    )
```
